32 devices in a mesh: replica: 8 (over z, y), tensor: 4 (over x, core).
Axes of the slice: x: 2, y: 2, z: 4, core: 2. Of those that a mesh axis runs over, the one named last changes fastest.
Arguments:
- attended: bfloat16 [8192, 8192], P('replica', 'tensor'), may hold values from -6 to 6
- out_weight: bfloat16 [8192, 8192], P('tensor'), may hold values from -0.09375 to 0.09375
- shrink_weight: bfloat16 [96, 64, 8192], P('replica', None, 'tensor'), may hold values from -0.0625 to 0.0625
- expand_weight: bfloat16 [96, 64, 8192], P('replica', None, 'tensor'), may hold values from -0.75 to 0.75
- block_adapter: int32 [64], P('replica'), may hold values from 0 to 95, as said below
- block_fill: int32 [64], P('replica'), may hold values from 1 to 128
Outputs:
- projected: bfloat16 [8192, 8192], P('replica', 'tensor')
The draws below stay inside these ranges and needn't reach their ends.
Inputs may be any that keep to these rules, and one draw needn't show every extreme that they name: `block_adapter`: the owner of adapter j is replica j // 12. Among the 8 blocks of one replica, at most 2 have adapters of one owner; one owner gets exactly 2 blocks from every replica.
All inputs are finite; a program needn't handle non-finite values.
Results may differ from the reference program's by a relative error of at most 0.02.
Values may be sent and summed in bfloat16 or wider, within the bound.
A program may use at most 128 MiB of HBM per device.

```python
import jax
import jax.numpy as jnp
from jax import lax

D = 8192
RANK = 64
BLOCK = 128
BLK_DEV = 8
CAP = 2
ADP_REP = 12
TOKENS = 8192
BLOCKS = 64
ADAPTERS = 96
N_TENSOR = 4


def draw_block_adapter(key, part):
    owner_count = ADAPTERS // ADP_REP
    replica_count = BLOCKS // BLK_DEV
    hot_key, rest_key = jax.random.split(jax.random.fold_in(key, 7))
    hot_rank = jax.random.permutation(hot_key, owner_count)
    replica_keys = jax.random.split(rest_key, replica_count)
    if CAP > 1:
        lowest = max(1, (BLK_DEV - owner_count + CAP - 2) // (CAP - 1))
    else:
        lowest = 1
    highest = max(lowest + 1, BLK_DEV // CAP + 1)

    def one_replica(replica_key):
        score_key, double_key, within_key = jax.random.split(replica_key, 3)
        scores = jax.random.randint(score_key, (owner_count,), 0, 4 * owner_count)
        scores = scores + jnp.where(hot_rank == 0, 8 * owner_count, 0) + jnp.where(hot_rank == 1, 3 * owner_count, 0)
        distinct = scores * owner_count + jnp.arange(owner_count)
        order = jnp.argsort(-distinct)
        doubles = jax.random.randint(double_key, (), lowest, highest)
        positions = jnp.arange(BLK_DEV)
        pattern = jnp.where(positions < CAP * doubles, positions // CAP, doubles + positions - CAP * doubles)
        owner_of = order[pattern]
        within = jax.random.randint(within_key, (BLK_DEV,), 0, ADP_REP)
        return owner_of * ADP_REP + within
    return jax.vmap(one_replica)(replica_keys).reshape(BLOCKS).astype(jnp.int32)


def touch_ends(entries, stream_key, low, largest):
    extent = entries.shape
    place = [jax.random.randint(jax.random.fold_in(stream_key, axis), (), 0, extent[axis]) for axis in range(len(extent))]
    entries = entries.at[tuple(place)].set(low)
    longest = extent.index(max(extent))
    place[longest] = (place[longest] + 1) % extent[longest]
    return entries.at[tuple(place)].set(largest)


def with_spikes(values, own_key, source, target, blocks, factor):
    def block_of(dim):
        return (jnp.arange(values.shape[dim]) // (values.shape[dim] // blocks)).reshape((-1,) + (1,) * (values.ndim - 1 - dim))

    one_side = jax.random.permutation(own_key, blocks)[block_of(target)]
    other_side = (block_of(target) + blocks // 2) % blocks
    return jnp.where((block_of(source) == one_side) | (block_of(source) == other_side), factor * values, values)


def level_of(key, extent, cuts, smallest, largest):
    factor_of, own = 1.0, jax.random.fold_in(key, 6)
    for axis_at, parts in cuts:
        steps = jnp.exp(jax.random.uniform(jax.random.fold_in(own, axis_at), (parts,), jnp.float32, smallest / len(cuts), largest / len(cuts)))
        factor_of = factor_of * jnp.repeat(steps, extent[axis_at] // parts).reshape([-1 if axis == axis_at else 1 for axis in range(len(extent))])
    return factor_of


def bell_draw(rng, dims, width, bound, cuts=(), kind=jnp.bfloat16):
    drawn = width * jax.random.normal(rng, dims, jnp.float32)
    if cuts:
        drawn = drawn * level_of(rng, dims, cuts, -0.22, 0.18)
    return jnp.clip(drawn, -bound, bound).astype(kind)


def noise_with(own_key, dims, width, most, shards, heavy, held_as=jnp.bfloat16):
    result = width * jax.random.normal(own_key, dims, jnp.float32)
    if shards:
        result = result * level_of(own_key, dims, shards, -0.22, 0.18)
    return jnp.clip(with_spikes(result, jax.random.fold_in(own_key, 3), *heavy), -most, most).astype(held_as)


def setup_inputs(seed: int = 0) -> dict:
    seeds = jax.random.split(jax.random.key(seed), 7)
    attended = bell_draw(seeds[0], (TOKENS, D), 1.0, 6.0, ((0, 8), (1, 4)))
    out_weight = noise_with(seeds[1], (D, D), D ** -0.5, 0.09375, ((0, 4),), (0, 1, 4, 2.0))
    shrink_weight = bell_draw(seeds[2], (ADAPTERS, RANK, D), D ** -0.5, 0.0625, ((0, 8), (2, 4)))
    expand_weight = bell_draw(seeds[3], (ADAPTERS, RANK, D), RANK ** -0.5, 0.75, ((0, 8), (2, 4)))
    block_adapter = draw_block_adapter(jax.random.fold_in(seeds[6], 71), 0)
    block_fill = touch_ends(jax.random.randint(seeds[5], (BLOCKS,), 1, BLOCK + 1), jax.random.fold_in(seeds[5], 1), 1, BLOCK).astype(jnp.int32)
    return dict(attended=attended, out_weight=out_weight, shrink_weight=shrink_weight, expand_weight=expand_weight, block_adapter=block_adapter, block_fill=block_fill)


def reference(attended, out_weight, shrink_weight, expand_weight, block_adapter, block_fill):
    feature_piece = D // N_TENSOR
    base_out = jnp.zeros((TOKENS, D), jnp.float32)
    for shard_index in range(N_TENSOR):
        columns = attended[:, shard_index * feature_piece:(shard_index + 1) * feature_piece]
        weight_rows = out_weight[shard_index * feature_piece:(shard_index + 1) * feature_piece, :]
        partial_out = jnp.dot(columns, weight_rows, preferred_element_type=jnp.float32).astype(jnp.bfloat16)
        partial_out = lax.optimization_barrier(partial_out)
        base_out = base_out + partial_out.astype(jnp.float32)
    block_count = TOKENS // BLOCK
    row_blocks = attended.reshape(block_count, BLOCK, D).astype(jnp.float32)
    shrink_sel = shrink_weight[block_adapter].astype(jnp.float32)
    low_rank = jnp.einsum("bcd,brd->bcr", row_blocks, shrink_sel).astype(jnp.bfloat16)
    low_rank = lax.optimization_barrier(low_rank)
    expand_sel = expand_weight[block_adapter].astype(jnp.float32)
    delta_rows = jnp.einsum("bcr,brd->bcd", low_rank.astype(jnp.float32), expand_sel).astype(jnp.bfloat16)
    delta_rows = lax.optimization_barrier(delta_rows)
    combined = base_out.reshape(block_count, BLOCK, D) + delta_rows.astype(jnp.float32)
    live_rows = jnp.arange(BLOCK, dtype=jnp.int32)[None, :] < block_fill[:, None]
    projected = jnp.where(live_rows[:, :, None], combined, 0.0).astype(jnp.bfloat16)
    return projected.reshape(TOKENS, D)
```

```python
import jax
import jax.numpy as jnp
from jax import lax
from jax.sharding import PartitionSpec as P


def slot_layout(block_ids, per_owner, capacity):
    block_owner = block_ids // per_owner
    local_ids = block_ids - block_owner * per_owner
    positions = jnp.arange(block_ids.shape[-1])
    earlier_same = (block_owner[..., None, :] == block_owner[..., :, None]) & (
        positions[None, :] < positions[:, None]
    )
    slot_rank = jnp.sum(earlier_same.astype(jnp.int32), axis=-1)
    return (block_owner * capacity + slot_rank, local_ids)


def local(attended, out_weight, shrink_weight, expand_weight, block_adapter, block_fill):
    tok_rows, feature_piece = attended.shape
    block_count = block_adapter.shape[0]
    block_rows = tok_rows // block_count
    rank = shrink_weight.shape[1]
    owner_count = lax.axis_size("replica")
    capacity = max(1, (2 * block_count + owner_count - 1) // owner_count)
    per_owner = shrink_weight.shape[0]
    slot_count = owner_count * capacity
    slot_index, local_ids = slot_layout(block_adapter, per_owner, capacity)
    block_table = lax.all_gather(block_adapter, "replica", axis=0, tiled=True).reshape(
        owner_count, block_count
    )
    all_slots, all_local = slot_layout(block_table, per_owner, capacity)
    wanted_slot = lax.axis_index("replica") * capacity + jnp.arange(capacity)
    served_hit = all_slots[:, None, :] == wanted_slot[None, :, None]
    served_ids = jnp.sum(jnp.where(served_hit, all_local[:, None, :], 0), axis=-1)
    both = jnp.concatenate([shrink_weight[served_ids], expand_weight[served_ids]], axis=2)
    arrived = lax.all_to_all(both, "replica", split_axis=0, concat_axis=0, tiled=True)
    arrived = arrived.reshape(slot_count, 2 * rank, feature_piece)
    partial_out = jnp.dot(attended, out_weight, preferred_element_type=jnp.float32)
    base_out = lax.psum_scatter(
        partial_out.astype(jnp.bfloat16), "tensor", scatter_dimension=1, tiled=True
    ).astype(jnp.float32)
    row_blocks = attended.reshape(block_count, block_rows, feature_piece)
    mine = arrived[slot_index]
    partial_low = jnp.einsum(
        "bcp,brp->bcr", row_blocks, mine[:, :rank], preferred_element_type=jnp.float32
    )
    low_rank = lax.psum(partial_low.astype(jnp.bfloat16), "tensor")
    delta_rows = jnp.einsum(
        "bcr,brp->bcp", low_rank, mine[:, rank:], preferred_element_type=jnp.float32
    ).astype(jnp.bfloat16)
    combined = base_out.reshape(block_count, block_rows, feature_piece) + delta_rows.astype(
        jnp.float32
    )
    live_rows = jnp.arange(block_rows)[None, :] < block_fill[:, None]
    projected = jnp.where(live_rows[:, :, None], combined, 0.0).astype(jnp.bfloat16)
    return projected.reshape(tok_rows, feature_piece)


def solution(mesh):
    in_specs = (
        P("replica", "tensor"),
        P("tensor", None),
        P("replica", None, "tensor"),
        P("replica", None, "tensor"),
        P("replica"),
        P("replica"),
    )
    out_specs = P("replica", "tensor")
    return jax.shard_map(local, mesh=mesh, in_specs=in_specs, out_specs=out_specs, check_vma=False)
```

```python
import functools

import jax
import jax.numpy as jnp
from jax import lax
from jax.experimental import pallas as pl
from jax.experimental.pallas import tpu as pltpu
from jax.sharding import PartitionSpec as P

MESH = pl.DeviceIdType.MESH
CHUNK = 512
ROW_TILE = 256


def kernel(R, T, cap, per, att_h, w_h, shrink_h, expand_h, tabin, ids, fill, out_h,
           att, shrink, expand, wbuf, tabv, tabs, stage_a, stage_e, recv_a, recv_e,
           psend, recvc, recvx, own, lowsend, lowrecv, low,
           load_sem, w_sem, tab_ssem, tab_rsem, tabs_sem, a_ssem, a_rsem, e_ssem, e_rsem,
           p_ssem, c_rsem, x_ssem, x_rsem, l_ssem, l_rsem, o_sem):
    me = lax.axis_index("replica")
    t = lax.axis_index("tensor")
    rows, f = att.shape
    B = ids.shape[0]
    blk = rows // B
    X = T // 2
    xc, c = t // 2, t % 2
    Q = f // CHUNK
    S = X * Q
    core_peer = t + 1 - 2 * c

    def w_copy(i, which):
        xo = lax.rem(xc + 1 + i // Q, X)
        piece = 2 * xo + (1 - c if which == 0 else c)
        col = pl.multiple_of(piece * f + lax.rem(i, Q) * CHUNK, CHUNK)
        return pltpu.make_async_copy(w_h.at[:, pl.ds(col, CHUNK)], wbuf.at[which], w_sem.at[which])

    att_load = pltpu.make_async_copy(att_h, att, load_sem.at[0])
    shrink_load = pltpu.make_async_copy(shrink_h, shrink, load_sem.at[1])
    expand_load = pltpu.make_async_copy(expand_h, expand, load_sem.at[2])
    shrink_load.start()
    expand_load.start()
    att_load.start()
    w_copy(0, 0).start()
    w_copy(0, 1).start()

    barrier = pltpu.get_barrier_semaphore()
    for k in range(1, R):
        pl.semaphore_signal(barrier, inc=1, device_id={"replica": lax.rem(me + k, R)}, device_id_type=MESH)
    for k in range(1, T):
        pl.semaphore_signal(barrier, inc=1, device_id={"tensor": lax.rem(t + k, T)}, device_id_type=MESH)
    pl.semaphore_wait(barrier, R + T - 2)

    def tab_copy(k):
        return pltpu.make_async_remote_copy(
            src_ref=tabin, dst_ref=tabv.at[me], send_sem=tab_ssem.at[k], recv_sem=tab_rsem.at[k],
            device_id={"replica": lax.rem(me + k, R)}, device_id_type=MESH)

    def adapter_copy(k, stage, recv, ssem, rsem):
        dst = lax.rem(me + k, R)
        return pltpu.make_async_remote_copy(
            src_ref=stage.at[dst], dst_ref=recv.at[me], send_sem=ssem.at[k], recv_sem=rsem.at[k],
            device_id={"replica": dst}, device_id_type=MESH)

    @pl.loop(1, R)
    def _(k):
        tab_copy(k).start()

    tabv[me] = tabin[...]

    @pl.loop(1, R)
    def _(k):
        tab_copy(k).wait()

    tab_local = pltpu.make_async_copy(tabv, tabs, tabs_sem)
    tab_local.start()
    tab_local.wait()

    def served(dst):
        count = jnp.int32(0)
        found = [jnp.int32(0) for _ in range(cap)]
        for b in range(B):
            local_id = tabs[dst, 0, b] - me * per
            mine = (local_id >= 0) & (local_id < per)
            for s in range(cap):
                found[s] = jnp.where(mine & (count == s), local_id, found[s])
            count = count + jnp.where(mine, 1, 0)
        return found

    def send_adapters(source, stage, recv, ssem, rsem):
        @pl.loop(1, R)
        def _(k):
            dst = lax.rem(me + k, R)
            for s, local_id in enumerate(served(dst)):
                stage[dst, s] = source[local_id]
            adapter_copy(k, stage, recv, ssem, rsem).start()

        for s, local_id in enumerate(served(me)):
            recv[me, s] = source[local_id]

    shrink_load.wait()
    send_adapters(shrink, stage_a, recv_a, a_ssem, a_rsem)
    expand_load.wait()
    send_adapters(expand, stage_e, recv_e, e_ssem, e_rsem)
    att_load.wait()

    def core_copy(i):
        slot = lax.rem(i, 2)
        return pltpu.make_async_remote_copy(
            src_ref=psend.at[slot], dst_ref=recvc.at[i], send_sem=p_ssem.at[slot], recv_sem=c_rsem.at[i],
            device_id={"tensor": core_peer}, device_id_type=MESH)

    def chip_copy(i):
        xo = lax.rem(xc + 1 + i // Q, X)
        return pltpu.make_async_remote_copy(
            src_ref=recvc.at[i], dst_ref=recvx.at[i], send_sem=x_ssem.at[i], recv_sem=x_rsem.at[i],
            device_id={"tensor": 2 * xo + c}, device_id_type=MESH)

    def product(which, tile):
        r = pl.ds(pl.multiple_of(tile * ROW_TILE, ROW_TILE), ROW_TILE)
        return r, jnp.dot(att[r, :], wbuf[which], preferred_element_type=jnp.float32)

    def for_peer(i):
        slot = lax.rem(i, 2)
        w_copy(i, 0).wait()

        @pl.when(i >= 2)
        def _():
            core_copy(i - 2).wait_send()

        @pl.loop(0, rows // ROW_TILE)
        def _(tile):
            r, value = product(0, tile)
            psend[slot, r, :] = value.astype(jnp.bfloat16)

        core_copy(i).start()

        @pl.when(i + 1 < S)
        def _():
            w_copy(i + 1, 0).start()

        w_copy(i, 1).wait()

    @pl.loop(0, S - Q)
    def _(i):
        for_peer(i)
        core_copy(i).wait_recv()

        @pl.loop(0, rows // ROW_TILE)
        def _(tile):
            r, value = product(1, tile)
            recvc[i, r, :] = (value + recvc[i, r, :].astype(jnp.float32)).astype(jnp.bfloat16)

        chip_copy(i).start()
        w_copy(i + 1, 1).start()

    @pl.loop(S - Q, S)
    def _(i):
        for_peer(i)
        col = pl.ds(pl.multiple_of((i - (S - Q)) * CHUNK, CHUNK), CHUNK)

        @pl.loop(0, rows // ROW_TILE)
        def _(tile):
            r, value = product(1, tile)
            own[r, col] = value.astype(jnp.bfloat16)

        @pl.when(i + 1 < S)
        def _():
            w_copy(i + 1, 1).start()

    @pl.loop(S - 2, S)
    def _(i):
        core_copy(i).wait_send()

    def place(b):
        owner = ids[b] // per
        slot = jnp.int32(0)
        for e in range(B):
            slot = slot + jnp.where((e < b) & (ids[e] // per == owner), 1, 0)
        return owner, jnp.minimum(slot, cap - 1)

    def low_copy(k):
        return pltpu.make_async_remote_copy(
            src_ref=lowsend, dst_ref=lowrecv.at[k], send_sem=l_ssem.at[k], recv_sem=l_rsem.at[k],
            device_id={"tensor": lax.rem(t + k, T)}, device_id_type=MESH)

    @pl.loop(1, R)
    def _(k):
        adapter_copy(k, stage_a, recv_a, a_ssem, a_rsem).wait()

    @pl.loop(0, B)
    def _(b):
        owner, slot = place(b)
        x_b = att[pl.ds(pl.multiple_of(b * blk, blk), blk), :]
        lowsend[b] = lax.dot_general(
            recv_a[owner, slot], x_b, (((1,), (1,)), ((), ())), preferred_element_type=jnp.float32
        ).astype(jnp.bfloat16)

    @pl.loop(1, T)
    def _(k):
        low_copy(k).start()

    @pl.loop(1, T)
    def _(k):
        low_copy(k).wait()

    @pl.loop(0, B)
    def _(b):
        total = lowsend[b].astype(jnp.float32)
        for k in range(1, T):
            total = total + lowrecv[k, b].astype(jnp.float32)
        low[b] = total.astype(jnp.bfloat16)

    @pl.loop(S - Q, S)
    def _(i):
        core_copy(i).wait_recv()

    @pl.loop(0, S - Q)
    def _(i):
        chip_copy(i).wait()

    @pl.loop(1, R)
    def _(k):
        adapter_copy(k, stage_e, recv_e, e_ssem, e_rsem).wait()

    def out_copy(b):
        r = pl.ds(pl.multiple_of(b * blk, blk), blk)
        return pltpu.make_async_copy(own.at[r, :], out_h.at[r, :], o_sem.at[b])

    @pl.loop(0, B)
    def _(b):
        owner, slot = place(b)
        r = pl.ds(pl.multiple_of(b * blk, blk), blk)
        live = lax.broadcasted_iota(jnp.int32, (blk, CHUNK), 0) < fill[b]
        for q in range(Q):
            cols = slice(q * CHUNK, (q + 1) * CHUNK)
            delta = lax.dot_general(
                low[b], recv_e[owner, slot, :, cols], (((0,), (0,)), ((), ())),
                preferred_element_type=jnp.float32).astype(jnp.bfloat16).astype(jnp.float32)
            base = own[r, cols].astype(jnp.float32) + recvc[S - Q + q, r, :].astype(jnp.float32)
            for j in range(X - 1):
                base = base + recvx[j * Q + q, r, :].astype(jnp.float32)
            own[r, cols] = jnp.where(live, base + delta, 0.0).astype(jnp.bfloat16)
        out_copy(b).start()

    @pl.loop(0, B)
    def _(b):
        out_copy(b).wait()


def local(R, T, attended, out_weight, shrink_weight, expand_weight, block_adapter, block_fill):
    rows, f = attended.shape
    B = block_adapter.shape[0]
    per, rank, _ = shrink_weight.shape
    cap = max(1, (2 * B + R - 1) // R)
    X = T // 2
    Q = f // CHUNK
    S = X * Q
    blk = rows // B
    tabin = jnp.broadcast_to(jnp.pad(block_adapter, (0, 128 - B))[None, :], (8, 128))
    bf = jnp.bfloat16
    dma = pltpu.SemaphoreType.DMA
    any_spec = pl.BlockSpec(memory_space=pl.ANY)
    return pl.pallas_call(
        functools.partial(kernel, R, T, cap, per),
        out_shape=jax.ShapeDtypeStruct((rows, f), bf),
        in_specs=[any_spec] * 4 + [pl.BlockSpec(memory_space=pltpu.VMEM)]
        + [pl.BlockSpec(memory_space=pltpu.SMEM)] * 2,
        out_specs=any_spec,
        scratch_shapes=[
            pltpu.VMEM((rows, f), bf),
            pltpu.VMEM((per, rank, f), bf),
            pltpu.VMEM((per, rank, f), bf),
            pltpu.VMEM((2, f, CHUNK), bf),
            pltpu.VMEM((R, 8, 128), jnp.int32),
            pltpu.SMEM((R, 8, 128), jnp.int32),
            pltpu.VMEM((R, cap, rank, f), bf),
            pltpu.VMEM((R, cap, rank, f), bf),
            pltpu.VMEM((R, cap, rank, f), bf),
            pltpu.VMEM((R, cap, rank, f), bf),
            pltpu.VMEM((2, rows, CHUNK), bf),
            pltpu.VMEM((S, rows, CHUNK), bf),
            pltpu.VMEM((S - Q, rows, CHUNK), bf),
            pltpu.VMEM((rows, f), bf),
            pltpu.VMEM((B, rank, blk), bf),
            pltpu.VMEM((T, B, rank, blk), bf),
            pltpu.VMEM((B, rank, blk), bf),
            dma((3,)), dma((2,)), dma((R,)), dma((R,)), dma,
            dma((R,)), dma((R,)), dma((R,)), dma((R,)),
            dma((2,)), dma((S,)), dma((S - Q,)), dma((S - Q,)), dma((T,)), dma((T,)), dma((B,)),
        ],
        compiler_params=pltpu.CompilerParams(
            collective_id=0, has_side_effects=True, vmem_limit_bytes=60 * 1024 * 1024
        ),
    )(attended, out_weight, shrink_weight, expand_weight, tabin, block_adapter, block_fill)


def solution(mesh):
    in_specs = (
        P("replica", "tensor"),
        P("tensor", None),
        P("replica", None, "tensor"),
        P("replica", None, "tensor"),
        P("replica"),
        P("replica"),
    )
    body = functools.partial(local, mesh.shape["replica"], mesh.shape["tensor"])
    return jax.shard_map(
        body, mesh=mesh, in_specs=in_specs, out_specs=P("replica", "tensor"), check_vma=False
    )
```

```python
import functools

import jax
import jax.numpy as jnp
from jax import lax
from jax.experimental import pallas as pl
from jax.experimental.pallas import tpu as pltpu
from jax.sharding import PartitionSpec as P

MESH = pl.DeviceIdType.MESH
CHUNK = 512
STRIDE = 5
ROW_TILE = 256


def kernel(R, T, cap, per, att_h, w_h, shrink_h, expand_h, ids, fill, out_h,
           att, shrink, expand, wbuf, tabin, tabv, tabs, stage_a, stage_e, recv_a, recv_e,
           psend, recvc, recvx, own, lowsend, lowrecv, low,
           load_sem, w_sem, tab_ssem, tab_rsem, tabs_sem, a_ssem, a_rsem, e_ssem, e_rsem,
           p_ssem, c_rsem, x_ssem, x_rsem, l_ssem, l_rsem, o_sem):
    me = lax.axis_index("replica")
    t = lax.axis_index("tensor")
    rows, f = att.shape
    B = ids.shape[0]
    blk = rows // B
    X = T // 2
    xc, c = t // 2, t % 2
    Q = f // CHUNK
    S = X * Q
    core_peer = t + 1 - 2 * c

    def w_copy(i, which):
        xo = lax.rem(xc + 1 + i // Q, X)
        piece = 2 * xo + (1 - c if which == 0 else c)
        col = pl.multiple_of(piece * f + lax.rem(i, Q) * CHUNK, CHUNK)
        return pltpu.make_async_copy(w_h.at[:, pl.ds(col, CHUNK)], wbuf.at[which], w_sem.at[which])

    att_load = pltpu.make_async_copy(att_h, att, load_sem.at[0])
    shrink_load = pltpu.make_async_copy(shrink_h, shrink, load_sem.at[1])
    expand_load = pltpu.make_async_copy(expand_h, expand, load_sem.at[2])
    shrink_load.start()
    expand_load.start()
    att_load.start()
    w_copy(0, 0).start()
    w_copy(0, 1).start()

    lane = lax.broadcasted_iota(jnp.int32, (8, 128), 1)
    table = jnp.zeros((8, 128), jnp.int32)
    for b in range(B):
        table = jnp.where(lane == b, ids[b], table)
    tabin[...] = table

    barrier = pltpu.get_barrier_semaphore()
    for k in range(1, R):
        pl.semaphore_signal(barrier, inc=1, device_id={"replica": lax.rem(me + k, R)}, device_id_type=MESH)
    for k in range(1, T):
        pl.semaphore_signal(barrier, inc=1, device_id={"tensor": lax.rem(t + k, T)}, device_id_type=MESH)
    pl.semaphore_wait(barrier, R + T - 2)

    def tab_copy(k):
        return pltpu.make_async_remote_copy(
            src_ref=tabin, dst_ref=tabv.at[me], send_sem=tab_ssem.at[k], recv_sem=tab_rsem.at[k],
            device_id={"replica": lax.rem(me + k, R)}, device_id_type=MESH)

    def adapter_copy(k, stage, recv, ssem, rsem):
        dst = lax.rem(me + STRIDE * k, R)
        return pltpu.make_async_remote_copy(
            src_ref=stage.at[dst], dst_ref=recv.at[me], send_sem=ssem.at[k], recv_sem=rsem.at[k],
            device_id={"replica": dst}, device_id_type=MESH)

    @pl.loop(1, R)
    def _(k):
        tab_copy(k).start()

    tabv[me] = table

    @pl.loop(1, R)
    def _(k):
        tab_copy(k).wait()

    tab_local = pltpu.make_async_copy(tabv, tabs, tabs_sem)
    tab_local.start()
    tab_local.wait()

    def served(dst):
        count = jnp.int32(0)
        found = [jnp.int32(0) for _ in range(cap)]
        for b in range(B):
            local_id = tabs[dst, 0, b] - me * per
            mine = (local_id >= 0) & (local_id < per)
            for s in range(cap):
                found[s] = jnp.where(mine & (count == s), local_id, found[s])
            count = count + jnp.where(mine, 1, 0)
        return found

    def send_adapters(source, stage, recv, ssem, rsem, cols=slice(None)):
        @pl.loop(1, R)
        def _(k):
            dst = lax.rem(me + STRIDE * k, R)
            for s, local_id in enumerate(served(dst)):
                stage[dst, s] = source[local_id, :, cols]
            adapter_copy(k, stage, recv, ssem, rsem).start()

        for s, local_id in enumerate(served(me)):
            recv[me, s] = source[local_id, :, cols]

    shrink_load.wait()
    send_adapters(shrink, stage_a, recv_a, a_ssem, a_rsem)
    expand_load.wait()
    att_load.wait()

    def core_copy(i):
        slot = lax.rem(i, 2)
        return pltpu.make_async_remote_copy(
            src_ref=psend.at[slot], dst_ref=recvc.at[i], send_sem=p_ssem.at[slot], recv_sem=c_rsem.at[i],
            device_id={"tensor": core_peer}, device_id_type=MESH)

    def chip_copy(i):
        xo = lax.rem(xc + 1 + i // Q, X)
        return pltpu.make_async_remote_copy(
            src_ref=recvc.at[i], dst_ref=recvx.at[i], send_sem=x_ssem.at[i], recv_sem=x_rsem.at[i],
            device_id={"tensor": 2 * xo + c}, device_id_type=MESH)

    def product(which, tile):
        r = pl.ds(pl.multiple_of(tile * ROW_TILE, ROW_TILE), ROW_TILE)
        return r, jnp.dot(att[r, :], wbuf[which], preferred_element_type=jnp.float32)

    def for_peer(i):
        slot = lax.rem(i, 2)
        w_copy(i, 0).wait()

        @pl.when(i >= 2)
        def _():
            core_copy(i - 2).wait_send()

        @pl.loop(0, rows // ROW_TILE)
        def _(tile):
            r, value = product(0, tile)
            psend[slot, r, :] = value.astype(jnp.bfloat16)

        core_copy(i).start()

        @pl.when(i + 1 < S)
        def _():
            w_copy(i + 1, 0).start()

        w_copy(i, 1).wait()

    @pl.loop(0, S - Q)
    def _(i):
        for_peer(i)
        core_copy(i).wait_recv()

        @pl.loop(0, rows // ROW_TILE)
        def _(tile):
            r, value = product(1, tile)
            recvc[i, r, :] = (value + recvc[i, r, :].astype(jnp.float32)).astype(jnp.bfloat16)

        chip_copy(i).start()
        w_copy(i + 1, 1).start()

    def send_expand(q):
        cols = slice(q * CHUNK, (q + 1) * CHUNK)
        send_adapters(expand, stage_e[q], recv_e[q], e_ssem.at[q], e_rsem.at[q], cols)

    for q in range(Q // 2):
        send_expand(q)

    @pl.loop(S - Q, S)
    def _(i):
        for_peer(i)
        col = pl.ds(pl.multiple_of((i - (S - Q)) * CHUNK, CHUNK), CHUNK)

        @pl.loop(0, rows // ROW_TILE)
        def _(tile):
            r, value = product(1, tile)
            own[r, col] = value.astype(jnp.bfloat16)

        @pl.when(i + 1 < S)
        def _():
            w_copy(i + 1, 1).start()

    @pl.loop(S - 2, S)
    def _(i):
        core_copy(i).wait_send()

    for q in range(Q // 2, Q):
        send_expand(q)

    def place(b):
        owner = ids[b] // per
        slot = jnp.int32(0)
        for e in range(B):
            slot = slot + jnp.where((e < b) & (ids[e] // per == owner), 1, 0)
        return owner, jnp.minimum(slot, cap - 1)

    def low_copy(k):
        return pltpu.make_async_remote_copy(
            src_ref=lowsend, dst_ref=lowrecv.at[k], send_sem=l_ssem.at[k], recv_sem=l_rsem.at[k],
            device_id={"tensor": lax.rem(t + k, T)}, device_id_type=MESH)

    @pl.loop(1, R)
    def _(k):
        adapter_copy(k, stage_a, recv_a, a_ssem, a_rsem).wait()

    @pl.loop(0, B)
    def _(b):
        owner, slot = place(b)
        x_b = att[pl.ds(pl.multiple_of(b * blk, blk), blk), :]
        lowsend[b] = lax.dot_general(
            recv_a[owner, slot], x_b, (((1,), (1,)), ((), ())), preferred_element_type=jnp.float32
        ).astype(jnp.bfloat16)

    @pl.loop(1, T)
    def _(k):
        low_copy(k).start()

    @pl.loop(1, T)
    def _(k):
        low_copy(k).wait()

    @pl.loop(0, B)
    def _(b):
        total = lowsend[b].astype(jnp.float32)
        for k in range(1, T):
            total = total + lowrecv[k, b].astype(jnp.float32)
        low[b] = total.astype(jnp.bfloat16)

    @pl.loop(S - Q, S)
    def _(i):
        core_copy(i).wait_recv()

    @pl.loop(0, S - Q)
    def _(i):
        chip_copy(i).wait()

    def out_copy(q):
        cols = pl.ds(q * CHUNK, CHUNK)
        return pltpu.make_async_copy(own.at[:, cols], out_h.at[:, cols], o_sem.at[q])

    for q in range(Q):
        cols = slice(q * CHUNK, (q + 1) * CHUNK)

        @pl.loop(1, R)
        def _(k):
            adapter_copy(k, stage_e[q], recv_e[q], e_ssem.at[q], e_rsem.at[q]).wait()

        @pl.loop(0, B)
        def _(b):
            owner, slot = place(b)
            r = pl.ds(pl.multiple_of(b * blk, blk), blk)
            live = lax.broadcasted_iota(jnp.int32, (blk, CHUNK), 0) < fill[b]
            delta = lax.dot_general(
                low[b], recv_e[q][owner, slot], (((0,), (0,)), ((), ())),
                preferred_element_type=jnp.float32).astype(jnp.bfloat16).astype(jnp.float32)
            base = own[r, cols].astype(jnp.float32) + recvc[S - Q + q, r, :].astype(jnp.float32)
            for j in range(X - 1):
                base = base + recvx[j * Q + q, r, :].astype(jnp.float32)
            own[r, cols] = jnp.where(live, base + delta, 0.0).astype(jnp.bfloat16)

        out_copy(q).start()

    for q in range(Q):
        out_copy(q).wait()


def local(R, T, attended, out_weight, shrink_weight, expand_weight, block_adapter, block_fill):
    rows, f = attended.shape
    B = block_adapter.shape[0]
    per, rank, _ = shrink_weight.shape
    cap = max(1, (2 * B + R - 1) // R)
    X = T // 2
    Q = f // CHUNK
    S = X * Q
    blk = rows // B
    bf = jnp.bfloat16
    dma = pltpu.SemaphoreType.DMA
    any_spec = pl.BlockSpec(memory_space=pl.ANY)
    return pl.pallas_call(
        functools.partial(kernel, R, T, cap, per),
        out_shape=jax.ShapeDtypeStruct((rows, f), bf),
        in_specs=[any_spec] * 4 + [pl.BlockSpec(memory_space=pltpu.SMEM)] * 2,
        out_specs=any_spec,
        scratch_shapes=[
            pltpu.VMEM((rows, f), bf),
            pltpu.VMEM((per, rank, f), bf),
            pltpu.VMEM((per, rank, f), bf),
            pltpu.VMEM((2, f, CHUNK), bf),
            pltpu.VMEM((8, 128), jnp.int32),
            pltpu.VMEM((R, 8, 128), jnp.int32),
            pltpu.SMEM((R, 8, 128), jnp.int32),
            pltpu.VMEM((R, cap, rank, f), bf),
            [pltpu.VMEM((R, cap, rank, CHUNK), bf) for _ in range(Q)],
            pltpu.VMEM((R, cap, rank, f), bf),
            [pltpu.VMEM((R, cap, rank, CHUNK), bf) for _ in range(Q)],
            pltpu.VMEM((2, rows, CHUNK), bf),
            pltpu.VMEM((S, rows, CHUNK), bf),
            pltpu.VMEM((S - Q, rows, CHUNK), bf),
            pltpu.VMEM((rows, f), bf),
            pltpu.VMEM((B, rank, blk), bf),
            pltpu.VMEM((T, B, rank, blk), bf),
            pltpu.VMEM((B, rank, blk), bf),
            dma((3,)), dma((2,)), dma((R,)), dma((R,)), dma,
            dma((R,)), dma((R,)), dma((Q, R)), dma((Q, R)),
            dma((2,)), dma((S,)), dma((S - Q,)), dma((S - Q,)), dma((T,)), dma((T,)), dma((Q,)),
        ],
        compiler_params=pltpu.CompilerParams(
            collective_id=0, has_side_effects=True, vmem_limit_bytes=60 * 1024 * 1024
        ),
    )(attended, out_weight, shrink_weight, expand_weight, block_adapter, block_fill)


def solution(mesh):
    in_specs = (
        P("replica", "tensor"),
        P("tensor", None),
        P("replica", None, "tensor"),
        P("replica", None, "tensor"),
        P("replica"),
        P("replica"),
    )
    body = functools.partial(local, mesh.shape["replica"], mesh.shape["tensor"])
    return jax.shard_map(
        body, mesh=mesh, in_specs=in_specs, out_specs=P("replica", "tensor"), check_vma=False
    )
```

```python
import functools

import jax
import jax.numpy as jnp
from jax import lax
from jax.experimental import pallas as pl
from jax.experimental.pallas import tpu as pltpu
from jax.sharding import PartitionSpec as P

MESH = pl.DeviceIdType.MESH
CHUNK = 512
STRIDE = 1
ROW_TILE = 256


def kernel(R, T, cap, per, att_h, w_h, shrink_h, expand_h, ids, fill, out_h,
           att, shrink, expand, wbuf, tabin, tabv, tabs, stage_a, stage_e, recv_a, recv_e,
           psend, recvc, recvx, own, lowsend, lowrecv, low,
           load_sem, w_sem, tab_ssem, tab_rsem, tabs_sem, a_ssem, a_rsem, e_ssem, e_rsem,
           p_ssem, c_rsem, x_ssem, x_rsem, l_ssem, l_rsem, o_sem):
    me = lax.axis_index("replica")
    t = lax.axis_index("tensor")
    rows, f = att.shape
    B = ids.shape[0]
    blk = rows // B
    X = T // 2
    xc, c = t // 2, t % 2
    Q = f // CHUNK
    S = X * Q
    core_peer = t + 1 - 2 * c

    def w_copy(i, which):
        xo = lax.rem(xc + 1 + i // Q, X)
        piece = 2 * xo + (1 - c if which == 0 else c)
        col = pl.multiple_of(piece * f + lax.rem(i, Q) * CHUNK, CHUNK)
        return pltpu.make_async_copy(w_h.at[:, pl.ds(col, CHUNK)], wbuf.at[which], w_sem.at[which])

    att_load = pltpu.make_async_copy(att_h, att, load_sem.at[0])
    shrink_load = pltpu.make_async_copy(shrink_h, shrink, load_sem.at[1])
    expand_load = pltpu.make_async_copy(expand_h, expand, load_sem.at[2])
    shrink_load.start()
    expand_load.start()
    att_load.start()
    w_copy(0, 0).start()
    w_copy(0, 1).start()

    lane = lax.broadcasted_iota(jnp.int32, (8, 128), 1)
    table = jnp.zeros((8, 128), jnp.int32)
    for b in range(B):
        table = jnp.where(lane == b, ids[b], table)
    tabin[...] = table

    barrier = pltpu.get_barrier_semaphore()
    for k in range(1, R):
        pl.semaphore_signal(barrier, inc=1, device_id={"replica": lax.rem(me + k, R)}, device_id_type=MESH)
    for k in range(1, T):
        pl.semaphore_signal(barrier, inc=1, device_id={"tensor": lax.rem(t + k, T)}, device_id_type=MESH)
    pl.semaphore_wait(barrier, R + T - 2)

    def tab_copy(k):
        return pltpu.make_async_remote_copy(
            src_ref=tabin, dst_ref=tabv.at[me], send_sem=tab_ssem.at[k], recv_sem=tab_rsem.at[k],
            device_id={"replica": lax.rem(me + k, R)}, device_id_type=MESH)

    def adapter_copy(k, stage, recv, ssem, rsem):
        dst = lax.rem(me + STRIDE * k, R)
        return pltpu.make_async_remote_copy(
            src_ref=stage.at[dst], dst_ref=recv.at[me], send_sem=ssem.at[k], recv_sem=rsem.at[k],
            device_id={"replica": dst}, device_id_type=MESH)

    @pl.loop(1, R)
    def _(k):
        tab_copy(k).start()

    tabv[me] = table

    @pl.loop(1, R)
    def _(k):
        tab_copy(k).wait()

    tab_local = pltpu.make_async_copy(tabv, tabs, tabs_sem)
    tab_local.start()
    tab_local.wait()

    def served(dst):
        count = jnp.int32(0)
        found = [jnp.int32(0) for _ in range(cap)]
        for b in range(B):
            local_id = tabs[dst, 0, b] - me * per
            mine = (local_id >= 0) & (local_id < per)
            for s in range(cap):
                found[s] = jnp.where(mine & (count == s), local_id, found[s])
            count = count + jnp.where(mine, 1, 0)
        return found

    def send_adapters(source, stage, recv, ssem, rsem, cols=slice(None)):
        @pl.loop(1, R)
        def _(k):
            dst = lax.rem(me + STRIDE * k, R)
            for s, local_id in enumerate(served(dst)):
                stage[dst, s] = source[local_id, :, cols]
            adapter_copy(k, stage, recv, ssem, rsem).start()

        for s, local_id in enumerate(served(me)):
            recv[me, s] = source[local_id, :, cols]

    shrink_load.wait()
    send_adapters(shrink, stage_a, recv_a, a_ssem, a_rsem)
    expand_load.wait()
    att_load.wait()

    def core_copy(i):
        slot = lax.rem(i, 2)
        return pltpu.make_async_remote_copy(
            src_ref=psend.at[slot], dst_ref=recvc.at[i], send_sem=p_ssem.at[slot], recv_sem=c_rsem.at[i],
            device_id={"tensor": core_peer}, device_id_type=MESH)

    def chip_copy(i):
        xo = lax.rem(xc + 1 + i // Q, X)
        return pltpu.make_async_remote_copy(
            src_ref=recvc.at[i], dst_ref=recvx.at[i], send_sem=x_ssem.at[i], recv_sem=x_rsem.at[i],
            device_id={"tensor": 2 * xo + c}, device_id_type=MESH)

    def product(which, tile):
        r = pl.ds(pl.multiple_of(tile * ROW_TILE, ROW_TILE), ROW_TILE)
        return r, jnp.dot(att[r, :], wbuf[which], preferred_element_type=jnp.float32)

    def for_peer(i):
        slot = lax.rem(i, 2)
        w_copy(i, 0).wait()

        @pl.when(i >= 2)
        def _():
            core_copy(i - 2).wait_send()

        @pl.loop(0, rows // ROW_TILE)
        def _(tile):
            r, value = product(0, tile)
            psend[slot, r, :] = value.astype(jnp.bfloat16)

        core_copy(i).start()

        @pl.when(i + 1 < S)
        def _():
            w_copy(i + 1, 0).start()

        w_copy(i, 1).wait()

    @pl.loop(0, S - Q)
    def _(i):
        for_peer(i)
        core_copy(i).wait_recv()

        @pl.loop(0, rows // ROW_TILE)
        def _(tile):
            r, value = product(1, tile)
            recvc[i, r, :] = (value + recvc[i, r, :].astype(jnp.float32)).astype(jnp.bfloat16)

        chip_copy(i).start()
        w_copy(i + 1, 1).start()

    def send_expand(q):
        cols = slice(q * CHUNK, (q + 1) * CHUNK)
        send_adapters(expand, stage_e[q], recv_e[q], e_ssem.at[q], e_rsem.at[q], cols)

    for q in range(Q // 2):
        send_expand(q)

    @pl.loop(S - Q, S)
    def _(i):
        for_peer(i)
        col = pl.ds(pl.multiple_of((i - (S - Q)) * CHUNK, CHUNK), CHUNK)

        @pl.loop(0, rows // ROW_TILE)
        def _(tile):
            r, value = product(1, tile)
            own[r, col] = value.astype(jnp.bfloat16)

        @pl.when(i + 1 < S)
        def _():
            w_copy(i + 1, 1).start()

    @pl.loop(S - 2, S)
    def _(i):
        core_copy(i).wait_send()

    for q in range(Q // 2, Q):
        send_expand(q)

    def place(b):
        owner = ids[b] // per
        slot = jnp.int32(0)
        for e in range(B):
            slot = slot + jnp.where((e < b) & (ids[e] // per == owner), 1, 0)
        return owner, jnp.minimum(slot, cap - 1)

    def low_copy(k):
        return pltpu.make_async_remote_copy(
            src_ref=lowsend, dst_ref=lowrecv.at[k], send_sem=l_ssem.at[k], recv_sem=l_rsem.at[k],
            device_id={"tensor": lax.rem(t + k, T)}, device_id_type=MESH)

    @pl.loop(1, R)
    def _(k):
        adapter_copy(k, stage_a, recv_a, a_ssem, a_rsem).wait()

    @pl.loop(0, B)
    def _(b):
        owner, slot = place(b)
        x_b = att[pl.ds(pl.multiple_of(b * blk, blk), blk), :]
        lowsend[b] = lax.dot_general(
            recv_a[owner, slot], x_b, (((1,), (1,)), ((), ())), preferred_element_type=jnp.float32
        ).astype(jnp.bfloat16)

    @pl.loop(1, T)
    def _(k):
        low_copy(k).start()

    @pl.loop(1, T)
    def _(k):
        low_copy(k).wait()

    @pl.loop(0, B)
    def _(b):
        total = lowsend[b].astype(jnp.float32)
        for k in range(1, T):
            total = total + lowrecv[k, b].astype(jnp.float32)
        low[b] = total.astype(jnp.bfloat16)

    @pl.loop(S - Q, S)
    def _(i):
        core_copy(i).wait_recv()

    @pl.loop(0, S - Q)
    def _(i):
        chip_copy(i).wait()

    def out_copy(q):
        cols = pl.ds(q * CHUNK, CHUNK)
        return pltpu.make_async_copy(own.at[:, cols], out_h.at[:, cols], o_sem.at[q])

    for q in range(Q):
        cols = slice(q * CHUNK, (q + 1) * CHUNK)

        @pl.loop(1, R)
        def _(k):
            adapter_copy(k, stage_e[q], recv_e[q], e_ssem.at[q], e_rsem.at[q]).wait()

        @pl.loop(0, B)
        def _(b):
            owner, slot = place(b)
            r = pl.ds(pl.multiple_of(b * blk, blk), blk)
            live = lax.broadcasted_iota(jnp.int32, (blk, CHUNK), 0) < fill[b]
            delta = lax.dot_general(
                low[b], recv_e[q][owner, slot], (((0,), (0,)), ((), ())),
                preferred_element_type=jnp.float32).astype(jnp.bfloat16).astype(jnp.float32)
            base = own[r, cols].astype(jnp.float32) + recvc[S - Q + q, r, :].astype(jnp.float32)
            for j in range(X - 1):
                base = base + recvx[j * Q + q, r, :].astype(jnp.float32)
            own[r, cols] = jnp.where(live, base + delta, 0.0).astype(jnp.bfloat16)

        out_copy(q).start()

    for q in range(Q):
        out_copy(q).wait()


def local(R, T, attended, out_weight, shrink_weight, expand_weight, block_adapter, block_fill):
    rows, f = attended.shape
    B = block_adapter.shape[0]
    per, rank, _ = shrink_weight.shape
    cap = max(1, (2 * B + R - 1) // R)
    X = T // 2
    Q = f // CHUNK
    S = X * Q
    blk = rows // B
    bf = jnp.bfloat16
    dma = pltpu.SemaphoreType.DMA
    any_spec = pl.BlockSpec(memory_space=pl.ANY)
    return pl.pallas_call(
        functools.partial(kernel, R, T, cap, per),
        out_shape=jax.ShapeDtypeStruct((rows, f), bf),
        in_specs=[any_spec] * 4 + [pl.BlockSpec(memory_space=pltpu.SMEM)] * 2,
        out_specs=any_spec,
        scratch_shapes=[
            pltpu.VMEM((rows, f), bf),
            pltpu.VMEM((per, rank, f), bf),
            pltpu.VMEM((per, rank, f), bf),
            pltpu.VMEM((2, f, CHUNK), bf),
            pltpu.VMEM((8, 128), jnp.int32),
            pltpu.VMEM((R, 8, 128), jnp.int32),
            pltpu.SMEM((R, 8, 128), jnp.int32),
            pltpu.VMEM((R, cap, rank, f), bf),
            [pltpu.VMEM((R, cap, rank, CHUNK), bf) for _ in range(Q)],
            pltpu.VMEM((R, cap, rank, f), bf),
            [pltpu.VMEM((R, cap, rank, CHUNK), bf) for _ in range(Q)],
            pltpu.VMEM((2, rows, CHUNK), bf),
            pltpu.VMEM((S, rows, CHUNK), bf),
            pltpu.VMEM((S - Q, rows, CHUNK), bf),
            pltpu.VMEM((rows, f), bf),
            pltpu.VMEM((B, rank, blk), bf),
            pltpu.VMEM((T, B, rank, blk), bf),
            pltpu.VMEM((B, rank, blk), bf),
            dma((3,)), dma((2,)), dma((R,)), dma((R,)), dma,
            dma((R,)), dma((R,)), dma((Q, R)), dma((Q, R)),
            dma((2,)), dma((S,)), dma((S - Q,)), dma((S - Q,)), dma((T,)), dma((T,)), dma((Q,)),
        ],
        compiler_params=pltpu.CompilerParams(
            collective_id=0, has_side_effects=True, vmem_limit_bytes=60 * 1024 * 1024
        ),
    )(attended, out_weight, shrink_weight, expand_weight, block_adapter, block_fill)


def solution(mesh):
    in_specs = (
        P("replica", "tensor"),
        P("tensor", None),
        P("replica", None, "tensor"),
        P("replica", None, "tensor"),
        P("replica"),
        P("replica"),
    )
    body = functools.partial(local, mesh.shape["replica"], mesh.shape["tensor"])
    return jax.shard_map(
        body, mesh=mesh, in_specs=in_specs, out_specs=P("replica", "tensor"), check_vma=False
    )
```
